512 devices in a mesh: dp: 4 (over x), tm: 16 (over y, core), head: 8 (over z).
Axes of the slice: x: 4, y: 8, z: 8, core: 2. Of those that a mesh axis runs over, the one named last changes fastest.
Arguments:
- queries: bfloat16 [512, 32, 3072], P(('dp', 'tm'), None, 'head'), parts along dimension 0, may hold values from -16 to 16
- keys: bfloat16 [512, 32, 3072], P(('dp', 'tm'), None, 'head'), parts along dimension 0, may hold values from -16 to 16
- values: bfloat16 [512, 32, 3072], P(('dp', 'tm'), None, 'head'), parts along dimension 0, may hold values from -6 to 6
- out_grad: bfloat16 [512, 32, 3072], P(('dp', 'tm'), None, 'head'), parts along dimension 0, may hold values from -6 to 6
- out_weight: bfloat16 [3072, 3072], P('tm', 'head'), may hold values from -0.109375 to 0.109375
- lists: int32 [128, 8], P(('dp', 'tm')), parts along dimension 0, may hold values from 0 to 127, as said below
Outputs:
- query_grad: bfloat16 [512, 32, 3072], P(('dp', 'tm'), None, 'head'), parts along dimension 0
- key_grad: bfloat16 [512, 32, 3072], P(('dp', 'tm'), None, 'head'), parts along dimension 0
- value_grad: bfloat16 [512, 32, 3072], P(('dp', 'tm'), None, 'head'), parts along dimension 0
- weight_grad: float32 [12288, 3072], P(('dp', 'tm'), 'head'), parts along dimension 0
The draws below stay inside these ranges and needn't reach their ends.
There are 4 independent parts, one for each index of `dp`. The reference program is written for one: setup_inputs(seed, part) draws one part's arguments, and reference() takes and returns one part's arrays. A program takes and returns all parts, laid end to end along the dimension named above; an argument that names none is the same for every part. Nothing has to cross between parts.
Inputs may be any that keep to these rules, and one draw needn't show every extreme that they name: `lists`: each group names 8 different frames of its rollout. Among the 16 list entries of one time shard's groups, at most 2 name frames owned by any one time shard, and those name at most 1 distinct frame; in every draw, every time shard has some owner for which both bounds are reached.
All inputs are finite; a program needn't handle non-finite values.
Results may differ from the reference program's by a relative error of at most 0.039.
Values may be sent and summed in bfloat16 or wider, within the bound.
No kernel may reach another device: no remote copies, remote signals or barrier semaphores. Data moves between devices by JAX's collectives and lax.ppermute only.
A program may use at most 64 MiB of HBM per device.

```python
import jax
import jax.numpy as jnp
from jax import lax

HEADS = 24
HD = 128
D = 3072
FTOK = 32
CF = 4
GROUPS_DEV = 2
RET = 8
HF = 3072
FR_DEV = 8
FRAMES = 128
GROUPS = 32
N_TM = 16


def draw_queries(key, part):
    own_key = jax.random.fold_in(key, 5)
    shape = (FRAMES, FTOK, HEADS * HD)
    return jnp.clip(jax.random.normal(own_key, shape, jnp.float32), -6.0, 6.0).astype(jnp.bfloat16)


def draw_keys(key, part):
    own_key = jax.random.fold_in(key, 7)
    shape = (FRAMES, FTOK, HEADS * HD)
    return jnp.clip(jax.random.normal(own_key, shape, jnp.float32), -6.0, 6.0).astype(jnp.bfloat16)


def draw_lists(key, part):
    key = jax.random.fold_in(key, 11)
    key_start, key_base = jax.random.split(key)
    per_owner = max(1, RET // N_TM)
    spread = FR_DEV // per_owner
    start_owner = jax.random.randint(key_start, (), 0, N_TM)
    base_frame = jax.random.randint(key_base, (N_TM, N_TM), 0, spread)
    group_ids = jnp.arange(GROUPS, dtype=jnp.int32)
    device_ids = group_ids // GROUPS_DEV
    within = group_ids % GROUPS_DEV
    entry_ids = jnp.arange(RET, dtype=jnp.int32)
    offset = within[:, None] * (RET // 2) + entry_ids[None, :]
    owner_ids = (start_owner + offset) % N_TM
    repeat = offset // N_TM % per_owner
    local_ids = base_frame[device_ids[:, None], owner_ids] + repeat * spread
    return (owner_ids * FR_DEV + local_ids).astype(jnp.int32)


def strengthened(drawn, key, source, target, blocks, factor):
    def block_of(dim):
        return (jnp.arange(drawn.shape[dim]) // (drawn.shape[dim] // blocks)).reshape((-1,) + (1,) * (drawn.ndim - 1 - dim))

    near = jax.random.permutation(key, blocks)[block_of(target)]
    other_side = (block_of(target) + blocks // 2) % blocks
    return jnp.where((block_of(source) == near) | (block_of(source) == other_side), factor * drawn, drawn)


def steps_of(key, extent, shards, least, high):
    gain = 1.0
    for dim, blocks in shards:
        draws = jax.random.uniform(jax.random.fold_in(jax.random.fold_in(key, 6), dim), (blocks,), jnp.float32, least / len(shards), high / len(shards))
        gain = gain * jnp.repeat(jnp.exp(draws), extent[dim] // blocks).reshape((-1,) + (1,) * (len(extent) - 1 - dim))
    return gain


def scatter_about(key, dims, scale, limit, cuts=(), kind=jnp.bfloat16):
    factor_of = steps_of(key, dims, cuts, -0.22, 0.18) if cuts else 1.0
    values = jax.random.normal(key, dims, jnp.float32) * scale * factor_of
    return jnp.minimum(jnp.maximum(values, -limit), limit).astype(kind)


def bell_draw_with(rng, shape, deviation, most, pieces, heavy, kind=jnp.bfloat16):
    drawn = deviation * jax.random.normal(rng, shape, jnp.float32)
    if pieces:
        drawn = drawn * steps_of(rng, shape, pieces, -0.22, 0.18)
    return jnp.clip(strengthened(drawn, jax.random.fold_in(rng, 3), *heavy), -most, most).astype(kind)


def setup_inputs(seed: int = 0, part: int = 0) -> dict:
    seeds = jax.random.split(jax.random.key(seed), 7)
    part_splits = jax.random.split(jax.random.fold_in(seeds[6], part), 7)
    return {
        "queries": draw_queries(jax.random.fold_in(jax.random.fold_in(seeds[6], part), 71), part),
        "keys": draw_keys(jax.random.fold_in(jax.random.fold_in(seeds[6], part), 71), part),
        "values": scatter_about(part_splits[2], (FRAMES, FTOK, HF), 1.0, 6.0, ((0, 16), (2, 8))),
        "out_grad": bell_draw_with(part_splits[3], (FRAMES, FTOK, D), 1.0, 6.0, ((0, 16), (2, 8)), (0, 2, 16, 2.0)),
        "out_weight": scatter_about(seeds[4], (D, HF), HF ** -0.5, 0.109375, ((0, 16), (1, 8))),
        "lists": draw_lists(jax.random.fold_in(jax.random.fold_in(seeds[6], part), 71), part),
    }


def rounded(array):
    return lax.optimization_barrier(array.astype(jnp.bfloat16)).astype(jnp.float32)


def group_backward(query_rows, own_keys, own_values, far_keys, far_values, grad_rows):
    factor = HD ** -0.5
    key_set = jnp.concatenate([own_keys, far_keys], axis=0).astype(jnp.float32)
    value_set = jnp.concatenate([own_values, far_values], axis=0).astype(jnp.float32)
    query_set = query_rows.astype(jnp.float32)
    grad_set = grad_rows.astype(jnp.float32)
    scores = jnp.einsum("qhd,khd->hqk", query_set, key_set) * factor
    row_top = jnp.max(scores, axis=2, keepdims=True)
    weighted = jnp.exp(scores - row_top)
    prob = weighted / jnp.sum(weighted, axis=2, keepdims=True)
    prob_low = rounded(prob)
    attn_out = rounded(jnp.einsum("hqk,khd->qhd", prob_low, value_set))
    row_dot = jnp.sum(grad_set * attn_out, axis=2)
    prob_grad = jnp.einsum("qhd,khd->hqk", grad_set, value_set)
    score_grad = rounded(prob * (prob_grad - jnp.transpose(row_dot)[:, :, None]))
    query_grad = (jnp.einsum("hqk,khd->qhd", score_grad, key_set) * factor).astype(jnp.bfloat16)
    key_term = jnp.einsum("hqk,qhd->khd", score_grad, query_set) * factor
    value_term = jnp.einsum("hqk,qhd->khd", prob_low, grad_set)
    return attn_out.astype(jnp.bfloat16), query_grad, key_term, value_term


def reference(queries, keys, values, out_grad, out_weight, lists):
    group_rows = CF * FTOK
    grad_flat = out_grad.reshape(FRAMES * FTOK, D)
    attn_grad = jnp.dot(grad_flat, out_weight, preferred_element_type=jnp.float32).astype(jnp.bfloat16)
    attn_grad = attn_grad.reshape(FRAMES, FTOK, HF)

    def one_group(group_inputs):
        group_id, picks = group_inputs
        first_frame = (group_id * CF).astype(jnp.int32)
        own_q = lax.dynamic_slice_in_dim(queries, first_frame, CF, 0).reshape(group_rows, HEADS, HD)
        own_k = lax.dynamic_slice_in_dim(keys, first_frame, CF, 0).reshape(group_rows, HEADS, HD)
        own_v = lax.dynamic_slice_in_dim(values, first_frame, CF, 0).reshape(group_rows, HEADS, HD)
        own_g = lax.dynamic_slice_in_dim(attn_grad, first_frame, CF, 0).reshape(group_rows, HEADS, HD)
        far_k = jnp.take(keys, picks.astype(jnp.int32), axis=0).reshape(RET * FTOK, HEADS, HD)
        far_v = jnp.take(values, picks.astype(jnp.int32), axis=0).reshape(RET * FTOK, HEADS, HD)
        return group_backward(own_q, own_k, own_v, far_k, far_v, own_g)

    attn_all, query_grad, key_term, value_term = lax.map(one_group, (jnp.arange(GROUPS, dtype=jnp.int32), lists))
    entry_count = GROUPS_DEV * RET
    wanted = lists.reshape(N_TM, entry_count).astype(jnp.int32)
    same_frame = wanted[:, :, None] == wanted[:, None, :]
    position = jnp.arange(entry_count, dtype=jnp.int32)
    before = position[:, None] < position[None, :]
    first_seen = jnp.logical_not(jnp.any(same_frame & before[None], axis=1))
    same_float = same_frame.astype(jnp.float32)

    def gathered(terms):
        own_part = terms[:, :group_rows].reshape(FRAMES, FTOK * HF)
        far_part = terms[:, group_rows:].reshape(N_TM, entry_count, FTOK * HF)
        summed = jnp.einsum("rij,rjx->rix", same_float, far_part, precision=lax.Precision.HIGHEST)
        kept = jnp.where(first_seen[:, :, None], rounded(summed), jnp.zeros_like(summed))
        total = jnp.zeros((FRAMES, FTOK * HF), jnp.float32).at[wanted.reshape(-1)].add(kept.reshape(-1, FTOK * HF))
        return (own_part + total).astype(jnp.bfloat16).reshape(FRAMES, FTOK, HF)

    key_grad = gathered(key_term)
    value_grad = gathered(value_term)
    attn_shards = attn_all.reshape(N_TM, FR_DEV * FTOK, HF)
    grad_shards = grad_flat.reshape(N_TM, FR_DEV * FTOK, D)

    def add_shard(running, shard_pair):
        grad_rows, attn_rows = shard_pair
        term = lax.dot_general(grad_rows, attn_rows, (((0,), (0,)), ((), ())), preferred_element_type=jnp.float32)
        return running + rounded(term), None

    weight_grad, unused = lax.scan(add_shard, jnp.zeros((D, HF), jnp.float32), (grad_shards, attn_shards))
    return query_grad.reshape(FRAMES, FTOK, HF), key_grad, value_grad, weight_grad
```

```python
import functools

import jax
import jax.numpy as jnp
from jax import lax
from jax.experimental import pallas as pl
from jax.experimental.pallas import tpu as pltpu
from jax.sharding import PartitionSpec as P

HD = 128
CF = 4
RET = 8
BF = jnp.bfloat16
F32 = jnp.float32
VMEM = pl.BlockSpec(memory_space=pltpu.VMEM)
SMEM = pl.BlockSpec(memory_space=pltpu.SMEM)
PARAMS = pltpu.CompilerParams(vmem_limit_bytes=40 * 1024 * 1024)
NT = (((1,), (1,)), ((), ()))
NN = (((1,), (0,)), ((), ()))
TN = (((0,), (0,)), ((), ()))


def dot(a, b, dims):
    return lax.dot_general(a, b, dims, preferred_element_type=F32)


def pack_body(source, keys, values, out):
    for shard in range(out.shape[0]):
        frame = source[shard]
        out[shard, 0] = keys[frame]
        out[shard, 1] = values[frame]


def fill_sets(lookup, group, keys, values, got, key_set, value_set):
    tokens = keys.shape[1]
    for f in range(CF):
        rows = pl.ds(f * tokens, tokens)
        key_set[rows, :] = keys[group * CF + f]
        value_set[rows, :] = values[group * CF + f]
    for e in range(RET):
        rows = pl.ds((CF + e) * tokens, tokens)
        owner = lookup[group * RET + e]
        key_set[rows, :] = got[owner, 0]
        value_set[rows, :] = got[owner, 1]


def probabilities(query, key_set):
    scores = dot(query, key_set, NT) * (HD**-0.5)
    weighted = jnp.exp(scores - jnp.max(scores, axis=1, keepdims=True))
    return weighted * (1.0 / jnp.sum(weighted, axis=1, keepdims=True))


def forward_body(lookup, queries, keys, values, got, grad, attn, partial, key_set, value_set):
    frames, tokens, width = queries.shape
    group_rows = CF * tokens
    for group in range(frames // CF):
        fill_sets(lookup, group, keys, values, got, key_set, value_set)
        for head in range(width // HD):
            cols = pl.ds(head * HD, HD)
            query = queries[pl.ds(group * CF, CF), :, cols].reshape(group_rows, HD)
            low = probabilities(query, key_set[:, cols]).astype(BF)
            attn[pl.ds(group * group_rows, group_rows), cols] = dot(
                low, value_set[:, cols], NN
            ).astype(BF)
    chunks, _, chunk = grad.shape
    for c in range(chunks):
        partial[pl.ds(c * chunk, chunk), :] = dot(grad[c], attn[...], TN).astype(BF)


def backward_body(
    lookup, queries, keys, values, got, grad, weight, attn,
    query_grad, back, own_dk, own_dv,
    key_set, value_set, attn_grad, far_dk, far_dv,
):
    frames, tokens, width = queries.shape
    group_rows = CF * tokens
    chunks, _, chunk = grad.shape
    total = dot(grad[0], weight[pl.ds(0, chunk), :], NN)
    for c in range(1, chunks):
        total += dot(grad[c], weight[pl.ds(c * chunk, chunk), :], NN)
    attn_grad[...] = total.astype(BF)
    far_dk[...] = jnp.zeros_like(far_dk)
    far_dv[...] = jnp.zeros_like(far_dv)
    for group in range(frames // CF):
        fill_sets(lookup, group, keys, values, got, key_set, value_set)
        rows = pl.ds(group * group_rows, group_rows)
        for head in range(width // HD):
            cols = pl.ds(head * HD, HD)
            query = queries[pl.ds(group * CF, CF), :, cols].reshape(group_rows, HD)
            prob = probabilities(query, key_set[:, cols])
            low = prob.astype(BF)
            out_grad = attn_grad[rows, cols]
            row_dot = jnp.sum(
                out_grad.astype(F32) * attn[rows, cols].astype(F32), axis=1, keepdims=True
            )
            prob_grad = dot(out_grad, value_set[:, cols], NT)
            score_grad = (prob * (prob_grad - row_dot)).astype(BF)
            dq = (dot(score_grad, key_set[:, cols], NN) * (HD**-0.5)).astype(BF)
            query_grad[pl.ds(group * CF, CF), :, cols] = dq.reshape(CF, tokens, HD)
            dk = dot(score_grad, query, TN) * (HD**-0.5)
            dv = dot(low, out_grad, TN)
            own_dk[rows, cols] = dk[:group_rows]
            own_dv[rows, cols] = dv[:group_rows]
            for e in range(RET):
                owner = lookup[group * RET + e]
                at = slice((CF + e) * tokens, (CF + e + 1) * tokens)
                far_dk[owner, :, cols] += dk[at]
                far_dv[owner, :, cols] += dv[at]
    back[:, 0] = far_dk[...].astype(BF)
    back[:, 1] = far_dv[...].astype(BF)


def finish_body(source, came, own_dk, own_dv, key_grad, value_grad, acc_k, acc_v):
    frames, tokens, width = key_grad.shape
    acc_k[...] = own_dk[...].reshape(frames, tokens, width)
    acc_v[...] = own_dv[...].reshape(frames, tokens, width)
    for shard in range(came.shape[0]):
        frame = source[shard]
        acc_k[frame] += came[shard, 0].astype(F32)
        acc_v[frame] += came[shard, 1].astype(F32)
    key_grad[...] = acc_k[...].astype(BF)
    value_grad[...] = acc_v[...].astype(BF)


def per_device(queries, keys, values, out_grad, out_weight, lists):
    frames, tokens, width = queries.shape
    shards = lax.axis_size("tm")
    heads = lax.axis_size("head")
    rows = frames * tokens
    entries = lists.size
    shape = jax.ShapeDtypeStruct
    myself = lax.axis_index("tm")

    wanted = lax.all_gather(lists, "tm", axis=0, tiled=True).reshape(shards, entries)
    source = jnp.max(jnp.where(wanted // frames == myself, wanted % frames, 0), axis=1)
    lookup = lists.reshape(entries) // frames
    grad = lax.all_gather(out_grad.reshape(rows, width), "head", axis=0, tiled=False)
    weight = lax.all_gather(out_weight, "tm", axis=0, tiled=True)

    packed = pl.pallas_call(
        pack_body,
        out_shape=shape((shards, 2, tokens, width), BF),
        in_specs=[SMEM, VMEM, VMEM],
        out_specs=VMEM,
        compiler_params=PARAMS,
        name="pack",
    )(source, keys, values)
    got = lax.all_to_all(packed, "tm", split_axis=0, concat_axis=0, tiled=True)

    sets = [pltpu.VMEM(((CF + RET) * tokens, width), BF)] * 2
    attn, partial = pl.pallas_call(
        forward_body,
        out_shape=(shape((rows, width), BF), shape((heads * width, width), BF)),
        in_specs=[SMEM] + [VMEM] * 5,
        out_specs=(VMEM, VMEM),
        scratch_shapes=sets,
        compiler_params=PARAMS,
        name="forward",
    )(lookup, queries, keys, values, got, grad)
    weight_grad = lax.psum_scatter(partial, "tm", scatter_dimension=0, tiled=True)

    query_grad, back, own_dk, own_dv = pl.pallas_call(
        backward_body,
        out_shape=(
            shape((frames, tokens, width), BF),
            shape((shards, 2, tokens, width), BF),
            shape((rows, width), F32),
            shape((rows, width), F32),
        ),
        in_specs=[SMEM] + [VMEM] * 7,
        out_specs=(VMEM,) * 4,
        scratch_shapes=sets
        + [pltpu.VMEM((rows, width), BF)]
        + [pltpu.VMEM((shards, tokens, width), F32)] * 2,
        compiler_params=PARAMS,
        name="backward",
    )(lookup, queries, keys, values, got, grad, weight, attn)
    came = lax.all_to_all(back, "tm", split_axis=0, concat_axis=0, tiled=True)

    key_grad, value_grad = pl.pallas_call(
        finish_body,
        out_shape=(shape((frames, tokens, width), BF),) * 2,
        in_specs=[SMEM] + [VMEM] * 3,
        out_specs=(VMEM, VMEM),
        scratch_shapes=[pltpu.VMEM((frames, tokens, width), F32)] * 2,
        compiler_params=PARAMS,
        name="finish",
    )(source, came, own_dk, own_dv)
    return query_grad, key_grad, value_grad, weight_grad.astype(F32)


def solution(mesh):
    tokens = P(("dp", "tm"), None, "head")
    return jax.shard_map(
        per_device,
        mesh=mesh,
        in_specs=(tokens, tokens, tokens, tokens, P("tm", "head"), P(("dp", "tm"), None)),
        out_specs=(tokens, tokens, tokens, P(("dp", "tm"), "head")),
        check_vma=False,
    )
```

```python
import functools

import jax
import jax.numpy as jnp
from jax import lax
from jax.experimental import pallas as pl
from jax.experimental.pallas import tpu as pltpu
from jax.sharding import PartitionSpec as P

HD = 128
CF = 4
RET = 8
LIST_ROWS = 16
BF = jnp.bfloat16
F32 = jnp.float32
HBM = pl.BlockSpec(memory_space=pltpu.HBM)
VMEM = pl.BlockSpec(memory_space=pltpu.VMEM)
SMEM = pl.BlockSpec(memory_space=pltpu.SMEM)
NT = (((1,), (1,)), ((), ()))
NN = (((1,), (0,)), ((), ()))
TN = (((0,), (0,)), ((), ()))


def dot(a, b, dims):
    return lax.dot_general(a, b, dims, preferred_element_type=F32)


def params():
    return pltpu.CompilerParams(vmem_limit_bytes=40 * 1024 * 1024)


def far(array):
    return pltpu.with_memory_space_constraint(array, pltpu.HBM)


def cost(flops, nbytes):
    return pl.CostEstimate(flops=flops, bytes_accessed=nbytes, transcendentals=0)


def pack_body(source, keys, values, out, sems):
    copies = []
    for shard in range(out.shape[0]):
        frame = source[shard]
        for which, held in enumerate((keys, values)):
            copy = pltpu.make_async_copy(
                held.at[frame], out.at[shard, which], sems.at[shard, which]
            )
            copy.start()
            copies.append(copy)
    for copy in copies:
        copy.wait()


def fill_sets(lookup, group, keys, values, got, key_set, value_set):
    tokens = keys.shape[1]
    for f in range(CF):
        rows = pl.ds(f * tokens, tokens)
        key_set[rows, :] = keys[group * CF + f]
        value_set[rows, :] = values[group * CF + f]
    for e in range(RET):
        rows = pl.ds((CF + e) * tokens, tokens)
        owner = lookup[group * RET + e]
        key_set[rows, :] = got[owner, 0]
        value_set[rows, :] = got[owner, 1]


def probabilities(query, key_set):
    scores = dot(query, key_set, NT) * (HD**-0.5)
    weighted = jnp.exp(scores - jnp.max(scores, axis=1, keepdims=True))
    return weighted * (1.0 / jnp.sum(weighted, axis=1, keepdims=True))


def forward_body(
    lookup, core, queries, keys, values, got, grad_far,
    probs, attn, keep, send,
    key_set, value_set, grad, sems,
):
    frames, tokens, width = queries.shape
    heads, group_rows = width // HD, CF * tokens
    chunks = grad.shape[0]
    copies = [
        pltpu.make_async_copy(grad_far.at[c], grad.at[c], sems.at[c]) for c in range(chunks)
    ]
    for copy in copies:
        copy.start()
    for g in range(frames // CF):
        fill_sets(lookup, g, keys, values, got, key_set, value_set)
        for h in range(heads):
            cols = pl.ds(h * HD, HD)
            query = queries[pl.ds(g * CF, CF), :, cols].reshape(group_rows, HD)
            prob = probabilities(query, key_set[:, cols])
            probs[g * heads + h] = prob
            attn[pl.ds(g * group_rows, group_rows), cols] = dot(
                prob.astype(BF), value_set[:, cols], NN
            ).astype(BF)
    first = core[0] == 0
    stripe = keep.shape[1]
    for c, copy in enumerate(copies):
        copy.wait()
        term = dot(grad[c], attn[...], TN).astype(BF)
        top, bottom = term[:stripe], term[stripe:]
        keep[c] = jnp.where(first, top, bottom)
        send[c] = jnp.where(first, bottom, top)


def add_body(ours, theirs, out, total, sems):
    copies = []
    for c in range(out.shape[0]):
        total[c] = (ours[c].astype(F32) + theirs[c].astype(F32)).astype(BF)
        copy = pltpu.make_async_copy(total.at[c], out.at[c], sems.at[c])
        copy.start()
        copies.append(copy)
    for copy in copies:
        copy.wait()


def backward_body(
    parts, lookup, place, queries, keys, values, got, probs, attn, grad_far, quarter, *refs
):
    pieces, refs = refs[: 2 * (parts - 1)], refs[2 * (parts - 1) :]
    query_grad, back, own_dk, own_dv = refs[:4]
    key_set, value_set, attn_grad, grad, weight = refs[4:9]
    far_dk, far_dv, held_dk, held_dv, gsems, wsems, osems = refs[9:]
    frames, tokens, width = queries.shape
    heads, group_rows = width // HD, CF * tokens
    chunks, _, chunk = grad.shape
    shards, _, rows, _ = weight.shape
    dp, core = place[0], place[1]
    half = shards // 2

    copies = [
        pltpu.make_async_copy(grad_far.at[c], grad.at[c], gsems.at[c]) for c in range(chunks)
    ]
    copies.append(
        pltpu.make_async_copy(quarter.at[:, pl.ds(0, rows)], weight.at[:, dp], wsems.at[0])
    )
    for i, piece in enumerate(pieces):
        origin = lax.rem(dp + parts - (1 + i // 2), parts)
        side = core if i % 2 == 0 else 1 - core
        copies.append(
            pltpu.make_async_copy(
                piece, weight.at[pl.ds(side * half, half), origin], wsems.at[1 + i]
            )
        )
    for copy in copies:
        copy.start()
    far_dk[...] = jnp.zeros_like(far_dk)
    far_dv[...] = jnp.zeros_like(far_dv)
    for copy in copies:
        copy.wait()
    per_chunk = chunk // (parts * rows)
    total = None
    for c in range(chunks):
        block = weight[pl.ds(c * per_chunk, per_chunk)].reshape(chunk, width)
        term = dot(grad[c], block, NN)
        total = term if total is None else total + term
    attn_grad[...] = total.astype(BF)

    copies = []
    for g in range(frames // CF):
        fill_sets(lookup, g, keys, values, got, key_set, value_set)
        mine = pl.ds(g * group_rows, group_rows)
        for h in range(heads):
            cols = pl.ds(h * HD, HD)
            query = queries[pl.ds(g * CF, CF), :, cols].reshape(group_rows, HD)
            prob = probs[g * heads + h]
            out_grad = attn_grad[mine, cols]
            row_dot = jnp.sum(
                out_grad.astype(F32) * attn[mine, cols].astype(F32), axis=1, keepdims=True
            )
            prob_grad = dot(out_grad, value_set[:, cols], NT)
            score_grad = (prob * (prob_grad - row_dot)).astype(BF)
            dq = (dot(score_grad, key_set[:, cols], NN) * (HD**-0.5)).astype(BF)
            query_grad[pl.ds(g * CF, CF), :, cols] = dq.reshape(CF, tokens, HD)
            dk = dot(score_grad, query, TN) * (HD**-0.5)
            dv = dot(prob.astype(BF), out_grad, TN)
            held_dk[mine, cols] = dk[:group_rows]
            held_dv[mine, cols] = dv[:group_rows]
            for e in range(RET):
                owner = lookup[g * RET + e]
                at = slice((CF + e) * tokens, (CF + e + 1) * tokens)
                far_dk[owner, :, cols] += dk[at]
                far_dv[owner, :, cols] += dv[at]
        for which, (held, out) in enumerate(((held_dk, own_dk), (held_dv, own_dv))):
            copy = pltpu.make_async_copy(held.at[mine], out.at[mine], osems.at[g, which])
            copy.start()
            copies.append(copy)
    back[:, 0] = far_dk[...].astype(BF)
    back[:, 1] = far_dv[...].astype(BF)
    for copy in copies:
        copy.wait()


def finish_body(source, came, own_dk, own_dv, key_grad, value_grad, acc_k, acc_v):
    frames, tokens, width = key_grad.shape
    acc_k[...] = own_dk[...].reshape(frames, tokens, width)
    acc_v[...] = own_dv[...].reshape(frames, tokens, width)
    for shard in range(came.shape[0]):
        frame = source[shard]
        acc_k[frame] += came[shard, 0].astype(F32)
        acc_v[frame] += came[shard, 1].astype(F32)
    key_grad[...] = acc_k[...].astype(BF)
    value_grad[...] = acc_v[...].astype(BF)


def per_device(queries, keys, values, out_grad, out_weight, lists):
    frames, tokens, width = queries.shape
    parts, chips = lax.axis_size("dp"), lax.axis_size("y")
    shards, heads = 2 * chips, lax.axis_size("head")
    dp, core = lax.axis_index("dp"), lax.axis_index("core")
    time = ("y", "core")
    myself = lax.axis_index(time)
    rows, entries, groups = frames * tokens, lists.size, frames // CF
    stripe = out_weight.shape[0]
    part_rows, half = stripe // parts, shards // 2
    shape = jax.ShapeDtypeStruct
    dma = pltpu.SemaphoreType.DMA
    other = [(0, 1), (1, 0)]

    grad = lax.all_gather(out_grad.reshape(rows, width), "head", axis=0, tiled=False)

    part = lax.dynamic_slice_in_dim(out_weight, dp * part_rows, part_rows, 0)
    names = jnp.zeros((LIST_ROWS, width), BF).at[0, :entries].set(lists.reshape(entries).astype(BF))
    quarter = lax.all_gather(jnp.concatenate([part, names], axis=0), time, axis=0, tiled=False)
    wanted = quarter[:, part_rows, :entries].astype(jnp.int32)
    source = jnp.max(jnp.where(wanted // frames == myself, wanted % frames, 0), axis=1)
    lookup = lists.reshape(entries) // frames

    packed = pl.pallas_call(
        pack_body,
        out_shape=shape((shards, 2, tokens, width), BF),
        in_specs=[SMEM, HBM, HBM],
        out_specs=HBM,
        scratch_shapes=[dma((shards, 2))],
        compiler_params=params(),
        cost_estimate=cost(0, 4 * shards * tokens * width * 2),
        name="pack",
    )(source, keys, values)
    got = lax.all_to_all(packed, time, split_axis=0, concat_axis=0, tiled=True)

    mine = lax.dynamic_slice_in_dim(quarter, core * half, half, 0)[:, :part_rows]
    halves = [
        lax.ppermute(mine, "dp", [(i, (i + s) % parts) for i in range(parts)])
        for s in range(1, parts)
    ]
    got, *halves = lax.optimization_barrier((got, *halves))
    pieces = []
    for piece in halves:
        pieces += [piece, lax.ppermute(piece, "core", other)]

    partial = shape((heads, stripe, width), BF)
    key_rows = (CF + RET) * tokens
    sets = pltpu.VMEM((key_rows, width), BF)
    chunks = pltpu.VMEM((heads, rows, width), BF)
    token_sum = pltpu.VMEM((rows, width), F32)
    far_sum = pltpu.VMEM((shards, tokens, width), F32)
    probs, attn, keep, send = pl.pallas_call(
        forward_body,
        out_shape=(
            shape((groups * width // HD, CF * tokens, key_rows), F32),
            shape((rows, width), BF),
            partial,
            partial,
        ),
        in_specs=[SMEM] * 2 + [VMEM] * 4 + [HBM],
        out_specs=(VMEM,) * 4,
        scratch_shapes=[sets, sets, chunks, dma((heads,))],
        compiler_params=params(),
        cost_estimate=cost(4 * 10**9, 8 * 10**6),
        name="forward",
    )(lookup, core[None], queries, keys, values, got, far(grad))

    theirs = lax.ppermute(send, "core", other)
    chip_sum = pl.pallas_call(
        add_body,
        out_shape=partial,
        in_specs=[VMEM, VMEM],
        out_specs=HBM,
        scratch_shapes=[pltpu.VMEM(partial.shape, BF), dma((heads,))],
        compiler_params=params(),
        cost_estimate=cost(10**6, 4 * 10**6),
        name="add",
    )(keep, theirs)
    weight_grad = lax.psum_scatter(chip_sum, "y", scatter_dimension=0, tiled=False)

    query_grad, back, own_dk, own_dv = pl.pallas_call(
        functools.partial(backward_body, parts),
        out_shape=(
            shape((frames, tokens, width), BF),
            shape((shards, 2, tokens, width), BF),
            shape((rows, width), F32),
            shape((rows, width), F32),
        ),
        in_specs=[SMEM] * 2 + [VMEM] * 6 + [HBM] * (2 + len(pieces)),
        out_specs=(VMEM, VMEM, HBM, HBM),
        scratch_shapes=[
            sets,
            sets,
            pltpu.VMEM((rows, width), BF),
            chunks,
            pltpu.VMEM((shards, parts, part_rows, width), BF),
            far_sum,
            far_sum,
            token_sum,
            token_sum,
            dma((heads,)),
            dma((1 + len(pieces),)),
            dma((groups, 2)),
        ],
        compiler_params=params(),
        cost_estimate=cost(6 * 10**9, 9 * 10**6),
        name="backward",
    )(
        lookup, jnp.stack([dp, core]), queries, keys, values, got, probs, attn,
        far(grad), far(quarter), *[far(p) for p in pieces],
    )
    came = lax.all_to_all(back, time, split_axis=0, concat_axis=0, tiled=True)

    key_grad, value_grad = pl.pallas_call(
        finish_body,
        out_shape=(shape((frames, tokens, width), BF),) * 2,
        in_specs=[SMEM] + [VMEM] * 3,
        out_specs=(VMEM, VMEM),
        scratch_shapes=[pltpu.VMEM((frames, tokens, width), F32)] * 2,
        compiler_params=params(),
        cost_estimate=cost(10**6, 3 * 10**6),
        name="finish",
    )(source, came, own_dk, own_dv)
    return query_grad, key_grad, value_grad, weight_grad.astype(F32)


def solution(mesh):
    dp, time, head = mesh.devices.shape
    fine = jax.sharding.Mesh(
        mesh.devices.reshape(dp, time // 2, 2, head), ("dp", "y", "core", "head")
    )
    tokens = P(("dp", "y", "core"), None, "head")
    return jax.shard_map(
        per_device,
        mesh=fine,
        in_specs=(
            tokens, tokens, tokens, tokens,
            P(("y", "core"), "head"),
            P(("dp", "y", "core"), None),
        ),
        out_specs=(tokens, tokens, tokens, P(("dp", "y", "core"), "head")),
        check_vma=False,
    )
```

```python
import functools

import jax
import jax.numpy as jnp
from jax import lax
from jax.experimental import pallas as pl
from jax.experimental.pallas import tpu as pltpu
from jax.sharding import PartitionSpec as P

HD = 128
CF = 4
RET = 8
LIST_ROWS = 16
BF = jnp.bfloat16
F32 = jnp.float32
HBM = pl.BlockSpec(memory_space=pltpu.HBM)
VMEM = pl.BlockSpec(memory_space=pltpu.VMEM)
SMEM = pl.BlockSpec(memory_space=pltpu.SMEM)
NT = (((1,), (1,)), ((), ()))
NN = (((1,), (0,)), ((), ()))
TN = (((0,), (0,)), ((), ()))


def dot(a, b, dims):
    return lax.dot_general(a, b, dims, preferred_element_type=F32)


def params():
    return pltpu.CompilerParams(vmem_limit_bytes=16 * 1024 * 1024)


def far(array):
    return pltpu.with_memory_space_constraint(array, pltpu.HBM)


def cost(flops, nbytes):
    return pl.CostEstimate(flops=flops, bytes_accessed=nbytes, transcendentals=0)


def pack_body(source, keys, values, out, sems):
    copies = []
    for shard in range(out.shape[0]):
        frame = source[shard]
        for which, held in enumerate((keys, values)):
            copy = pltpu.make_async_copy(
                held.at[frame], out.at[shard, which], sems.at[shard, which]
            )
            copy.start()
            copies.append(copy)
    for copy in copies:
        copy.wait()


def fill_sets(lookup, group, keys, values, got, key_set, value_set):
    tokens = keys.shape[1]
    for f in range(CF):
        rows = pl.ds(f * tokens, tokens)
        key_set[rows, :] = keys[group * CF + f]
        value_set[rows, :] = values[group * CF + f]
    for e in range(RET):
        rows = pl.ds((CF + e) * tokens, tokens)
        owner = lookup[group * RET + e]
        key_set[rows, :] = got[owner, 0]
        value_set[rows, :] = got[owner, 1]


def probabilities(query, key_set):
    scores = dot(query, key_set, NT) * (HD**-0.5)
    weighted = jnp.exp(scores - jnp.max(scores, axis=1, keepdims=True))
    return weighted * (1.0 / jnp.sum(weighted, axis=1, keepdims=True))


def attend_body(lookup, queries, keys, values, got, attn, key_set, value_set):
    frames, tokens, width = queries.shape
    heads, group_rows = width // HD, CF * tokens
    for g in range(frames // CF):
        fill_sets(lookup, g, keys, values, got, key_set, value_set)
        for h in range(heads):
            cols = pl.ds(h * HD, HD)
            query = queries[pl.ds(g * CF, CF), :, cols].reshape(group_rows, HD)
            low = probabilities(query, key_set[:, cols]).astype(BF)
            attn[pl.ds(g * group_rows, group_rows), cols] = dot(
                low, value_set[:, cols], NN
            ).astype(BF)


def term_body(side, grad, attn, out):
    stripe = out.shape[1]
    first = side[0] == 0
    for c in range(grad.shape[0]):
        block = jnp.where(first, grad[c, :, :stripe], grad[c, :, stripe:])
        out[c] = dot(block, attn[...], TN).astype(BF)


def add_body(ours, theirs, out, total, sems):
    copies = []
    for c in range(out.shape[0]):
        total[c] = (ours[c].astype(F32) + theirs[c].astype(F32)).astype(BF)
        copy = pltpu.make_async_copy(total.at[c], out.at[c], sems.at[c])
        copy.start()
        copies.append(copy)
    for copy in copies:
        copy.wait()


def join_body(*refs):
    out = refs[-1]
    for i, ref in enumerate(refs[:-1]):
        out[i] = ref[...]


def backward_body(
    parts, lookup, place, queries, keys, values, got, attn, grad_far, quarter, halves, sibling,
    query_grad, back, own_dk, own_dv,
    key_sets, value_sets, probs, attn_grad, grad, weight, far_dk, far_dv, held_dk, held_dv, gsems, osems,
):
    frames, tokens, width = queries.shape
    heads, group_rows = width // HD, CF * tokens
    chunks, _, chunk = grad.shape
    shards, _, rows, _ = weight.shape
    dp, core = place[0], place[1]
    half = shards // 2

    grad_copies = [
        pltpu.make_async_copy(grad_far.at[c], grad.at[c], gsems.at[c]) for c in range(chunks)
    ]
    for copy in grad_copies:
        copy.start()
    for g in range(frames // CF):
        fill_sets(lookup, g, keys, values, got, key_sets.at[g], value_sets.at[g])
        for h in range(heads):
            cols = pl.ds(h * HD, HD)
            query = queries[pl.ds(g * CF, CF), :, cols].reshape(group_rows, HD)
            probs[g * heads + h] = probabilities(query, key_sets[g, :, cols])
    weight[:, dp] = quarter[:, :rows]
    for i in range(parts - 1):
        origin = lax.rem(dp + parts - (1 + i), parts)
        weight[pl.ds(core * half, half), origin] = halves[i]
        weight[pl.ds((1 - core) * half, half), origin] = sibling[i]
    far_dk[...] = jnp.zeros_like(far_dk)
    far_dv[...] = jnp.zeros_like(far_dv)
    per_chunk = chunk // (parts * rows)
    total = None
    for c, copy in enumerate(grad_copies):
        copy.wait()
        block = weight[pl.ds(c * per_chunk, per_chunk)].reshape(chunk, width)
        term = dot(grad[c], block, NN)
        total = term if total is None else total + term
    attn_grad[...] = total.astype(BF)

    copies = []
    for g in range(frames // CF):
        mine = pl.ds(g * group_rows, group_rows)
        for h in range(heads):
            cols = pl.ds(h * HD, HD)
            query = queries[pl.ds(g * CF, CF), :, cols].reshape(group_rows, HD)
            prob = probs[g * heads + h]
            out_grad = attn_grad[mine, cols]
            row_dot = jnp.sum(
                out_grad.astype(F32) * attn[mine, cols].astype(F32), axis=1, keepdims=True
            )
            prob_grad = dot(out_grad, value_sets[g, :, cols], NT)
            score_grad = (prob * (prob_grad - row_dot)).astype(BF)
            dq = (dot(score_grad, key_sets[g, :, cols], NN) * (HD**-0.5)).astype(BF)
            query_grad[pl.ds(g * CF, CF), :, cols] = dq.reshape(CF, tokens, HD)
            dk = dot(score_grad, query, TN) * (HD**-0.5)
            dv = dot(prob.astype(BF), out_grad, TN)
            held_dk[mine, cols] = dk[:group_rows]
            held_dv[mine, cols] = dv[:group_rows]
            for e in range(RET):
                owner = lookup[g * RET + e]
                at = slice((CF + e) * tokens, (CF + e + 1) * tokens)
                far_dk[owner, :, cols] += dk[at]
                far_dv[owner, :, cols] += dv[at]
        for which, (held, out) in enumerate(((held_dk, own_dk), (held_dv, own_dv))):
            copy = pltpu.make_async_copy(held.at[mine], out.at[mine], osems.at[g, which])
            copy.start()
            copies.append(copy)
    back[:, 0] = far_dk[...].astype(BF)
    back[:, 1] = far_dv[...].astype(BF)
    for copy in copies:
        copy.wait()


def finish_body(source, came, own_dk, own_dv, key_grad, value_grad, acc_k, acc_v):
    frames, tokens, width = key_grad.shape
    acc_k[...] = own_dk[...].reshape(frames, tokens, width)
    acc_v[...] = own_dv[...].reshape(frames, tokens, width)
    for shard in range(came.shape[0]):
        frame = source[shard]
        acc_k[frame] += came[shard, 0].astype(F32)
        acc_v[frame] += came[shard, 1].astype(F32)
    key_grad[...] = acc_k[...].astype(BF)
    value_grad[...] = acc_v[...].astype(BF)


def per_device(queries, keys, values, out_grad, out_weight, lists):
    frames, tokens, width = queries.shape
    parts, chips = lax.axis_size("dp"), lax.axis_size("y")
    shards, heads = 2 * chips, lax.axis_size("head")
    dp, core = lax.axis_index("dp"), lax.axis_index("core")
    time = ("y", "core")
    myself = lax.axis_index(time)
    rows, entries, groups = frames * tokens, lists.size, frames // CF
    stripe = out_weight.shape[0]
    part_rows, half = stripe // parts, shards // 2
    shape = jax.ShapeDtypeStruct
    dma = pltpu.SemaphoreType.DMA
    other = [(0, 1), (1, 0)]

    grad = lax.all_gather(out_grad.reshape(rows, width), "head", axis=0, tiled=False)

    part = lax.dynamic_slice_in_dim(out_weight, dp * part_rows, part_rows, 0)
    names = jnp.zeros((LIST_ROWS, width), BF).at[0, :entries].set(lists.reshape(entries).astype(BF))
    quarter = lax.all_gather(jnp.concatenate([part, names], axis=0), time, axis=0, tiled=False)
    wanted = quarter[:, part_rows, :entries].astype(jnp.int32)
    source = jnp.max(jnp.where(wanted // frames == myself, wanted % frames, 0), axis=1)
    lookup = lists.reshape(entries) // frames

    packed = pl.pallas_call(
        pack_body,
        out_shape=shape((shards, 2, tokens, width), BF),
        in_specs=[SMEM, HBM, HBM],
        out_specs=HBM,
        scratch_shapes=[dma((shards, 2))],
        compiler_params=params(),
        cost_estimate=cost(0, 4 * shards * tokens * width * 2),
        name="pack",
    )(source, keys, values)
    got = lax.all_to_all(packed, time, split_axis=0, concat_axis=0, tiled=True)

    mine = lax.dynamic_slice_in_dim(quarter, core * half, half, 0)[:, :part_rows]
    halves = [
        lax.ppermute(mine, "dp", [(i, (i + s) % parts) for i in range(parts)])
        for s in range(1, parts)
    ]
    partial = shape((heads, stripe, width), BF)
    key_rows = (CF + RET) * tokens
    sets = pltpu.VMEM((key_rows, width), BF)
    token_sum = pltpu.VMEM((rows, width), F32)
    far_sum = pltpu.VMEM((shards, tokens, width), F32)
    attn = pl.pallas_call(
        attend_body,
        out_shape=shape((rows, width), BF),
        in_specs=[SMEM] + [VMEM] * 4,
        out_specs=VMEM,
        scratch_shapes=[sets, sets],
        compiler_params=params(),
        cost_estimate=cost(2 * 10**9, 8 * 10**6),
        name="attend",
    )(lookup, queries, keys, values, got)
    attn, *halves = lax.optimization_barrier((attn, *halves))

    def term(side, name):
        return pl.pallas_call(
            term_body,
            out_shape=partial,
            in_specs=[SMEM, VMEM, VMEM],
            out_specs=VMEM,
            compiler_params=params(),
            cost_estimate=cost(3 * 10**9, 3 * 10**6),
            name=name,
        )(side[None], grad, attn)

    send, keep = term(1 - core, "send"), term(core, "keep")
    theirs = lax.ppermute(send, "core", other)
    chip_sum = pl.pallas_call(
        add_body,
        out_shape=partial,
        in_specs=[VMEM, VMEM],
        out_specs=HBM,
        scratch_shapes=[pltpu.VMEM(partial.shape, BF), dma((heads,))],
        compiler_params=params(),
        cost_estimate=cost(10**6, 4 * 10**6),
        name="add",
    )(keep, theirs)
    halves = pl.pallas_call(
        join_body,
        out_shape=shape((parts - 1, half, part_rows, width), BF),
        in_specs=[VMEM] * (parts - 1),
        out_specs=VMEM,
        compiler_params=params(),
        cost_estimate=cost(0, 2 * 10**6),
        name="join",
    )(*halves)
    sibling = lax.ppermute(halves, "core", other)
    weight_grad = lax.psum_scatter(chip_sum, "y", scatter_dimension=0, tiled=False)

    query_grad, back, own_dk, own_dv = pl.pallas_call(
        functools.partial(backward_body, parts),
        out_shape=(
            shape((frames, tokens, width), BF),
            shape((shards, 2, tokens, width), BF),
            shape((rows, width), F32),
            shape((rows, width), F32),
        ),
        in_specs=[SMEM] * 2 + [VMEM] * 5 + [HBM] + [VMEM] * 3,
        out_specs=(VMEM, VMEM, HBM, HBM),
        scratch_shapes=[
            pltpu.VMEM((groups, key_rows, width), BF),
            pltpu.VMEM((groups, key_rows, width), BF),
            pltpu.VMEM((groups * width // HD, CF * tokens, key_rows), F32),
            pltpu.VMEM((rows, width), BF),
            pltpu.VMEM((heads, rows, width), BF),
            pltpu.VMEM((shards, parts, part_rows, width), BF),
            far_sum,
            far_sum,
            token_sum,
            token_sum,
            dma((heads,)),
            dma((groups, 2)),
        ],
        compiler_params=params(),
        cost_estimate=cost(6 * 10**9, 9 * 10**6),
        name="backward",
    )(
        lookup, jnp.stack([dp, core]), queries, keys, values, got, attn,
        far(grad), quarter, halves, sibling,
    )
    came = lax.all_to_all(back, time, split_axis=0, concat_axis=0, tiled=True)

    key_grad, value_grad = pl.pallas_call(
        finish_body,
        out_shape=(shape((frames, tokens, width), BF),) * 2,
        in_specs=[SMEM] + [VMEM] * 3,
        out_specs=(VMEM, VMEM),
        scratch_shapes=[pltpu.VMEM((frames, tokens, width), F32)] * 2,
        compiler_params=params(),
        cost_estimate=cost(10**6, 3 * 10**6),
        name="finish",
    )(source, came, own_dk, own_dv)
    return query_grad, key_grad, value_grad, weight_grad.astype(F32)


def solution(mesh):
    dp, time, head = mesh.devices.shape
    fine = jax.sharding.Mesh(
        mesh.devices.reshape(dp, time // 2, 2, head), ("dp", "y", "core", "head")
    )
    tokens = P(("dp", "y", "core"), None, "head")
    return jax.shard_map(
        per_device,
        mesh=fine,
        in_specs=(
            tokens, tokens, tokens, tokens,
            P(("y", "core"), "head"),
            P(("dp", "y", "core"), None),
        ),
        out_specs=(tokens, tokens, tokens, P(("dp", "y", "core"), "head")),
        check_vma=False,
    )
```

```python
import functools

import jax
import jax.numpy as jnp
from jax import lax
from jax.experimental import pallas as pl
from jax.experimental.pallas import tpu as pltpu
from jax.sharding import PartitionSpec as P

HD = 128
CF = 4
RET = 8
LIST_ROWS = 16
BF = jnp.bfloat16
F32 = jnp.float32
HBM = pl.BlockSpec(memory_space=pltpu.HBM)
VMEM = pl.BlockSpec(memory_space=pltpu.VMEM)
SMEM = pl.BlockSpec(memory_space=pltpu.SMEM)
NT = (((1,), (1,)), ((), ()))
NN = (((1,), (0,)), ((), ()))
TN = (((0,), (0,)), ((), ()))


def dot(a, b, dims):
    return lax.dot_general(a, b, dims, preferred_element_type=F32)


def params():
    return pltpu.CompilerParams(vmem_limit_bytes=16 * 1024 * 1024)


def far(array):
    return pltpu.with_memory_space_constraint(array, pltpu.HBM)


def cost(flops, nbytes):
    return pl.CostEstimate(flops=flops, bytes_accessed=nbytes, transcendentals=0)


def pack_body(source, keys, values, out, sems):
    copies = []
    for shard in range(out.shape[0]):
        frame = source[shard]
        for which, held in enumerate((keys, values)):
            copy = pltpu.make_async_copy(
                held.at[frame], out.at[shard, which], sems.at[shard, which]
            )
            copy.start()
            copies.append(copy)
    for copy in copies:
        copy.wait()


def fill_sets(lookup, group, keys, values, got, key_set, value_set):
    tokens = keys.shape[1]
    for f in range(CF):
        rows = pl.ds(f * tokens, tokens)
        key_set[rows, :] = keys[group * CF + f]
        value_set[rows, :] = values[group * CF + f]
    for e in range(RET):
        rows = pl.ds((CF + e) * tokens, tokens)
        owner = lookup[group * RET + e]
        key_set[rows, :] = got[owner, 0]
        value_set[rows, :] = got[owner, 1]


def probabilities(query, key_set):
    scores = dot(query, key_set, NT) * (HD**-0.5)
    weighted = jnp.exp(scores - jnp.max(scores, axis=1, keepdims=True))
    return weighted * (1.0 / jnp.sum(weighted, axis=1, keepdims=True))


def attend_body(lookup, queries, keys, values, got, attn, key_sets, value_sets):
    frames, tokens, width = queries.shape
    heads, group_rows = width // HD, CF * tokens
    for g in range(frames // CF):
        fill_sets(lookup, g, keys, values, got, key_sets.at[g], value_sets.at[g])
        for h in range(heads):
            cols = pl.ds(h * HD, HD)
            query = queries[pl.ds(g * CF, CF), :, cols].reshape(group_rows, HD)
            low = probabilities(query, key_sets[g, :, cols]).astype(BF)
            attn[pl.ds(g * group_rows, group_rows), cols] = dot(
                low, value_sets[g, :, cols], NN
            ).astype(BF)


def term_body(side, grad, attn, out):
    stripe = out.shape[1]
    first = side[0] == 0
    for c in range(grad.shape[0]):
        block = jnp.where(first, grad[c, :, :stripe], grad[c, :, stripe:])
        out[c] = dot(block, attn[...], TN).astype(BF)


def add_body(ours, theirs, out, total, sems):
    copies = []
    for c in range(out.shape[0]):
        total[c] = (ours[c].astype(F32) + theirs[c].astype(F32)).astype(BF)
        copy = pltpu.make_async_copy(total.at[c], out.at[c], sems.at[c])
        copy.start()
        copies.append(copy)
    for copy in copies:
        copy.wait()


def join_body(*refs):
    out = refs[-1]
    for i, ref in enumerate(refs[:-1]):
        out[i] = ref[...]


def backward_body(
    parts, lookup, place, queries, keys, values, got, attn, grad_far, quarter, halves, sibling,
    query_grad, back, own_dk, own_dv,
    key_sets, value_sets, probs, attn_grad, grad, weight, far_dk, far_dv, held_dk, held_dv, gsems, osems,
):
    frames, tokens, width = queries.shape
    heads, group_rows = width // HD, CF * tokens
    chunks, _, chunk = grad.shape
    shards, _, rows, _ = weight.shape
    dp, core = place[0], place[1]
    half = shards // 2

    grad_copies = [
        pltpu.make_async_copy(grad_far.at[c], grad.at[c], gsems.at[c]) for c in range(chunks)
    ]
    for copy in grad_copies:
        copy.start()
    for g in range(frames // CF):
        fill_sets(lookup, g, keys, values, got, key_sets.at[g], value_sets.at[g])
        for h in range(heads):
            cols = pl.ds(h * HD, HD)
            query = queries[pl.ds(g * CF, CF), :, cols].reshape(group_rows, HD)
            probs[g * heads + h] = probabilities(query, key_sets[g, :, cols])
    weight[:, dp] = quarter[:, :rows]
    for i in range(parts - 1):
        origin = lax.rem(dp + parts - (1 + i), parts)
        weight[pl.ds(core * half, half), origin] = halves[i]
        weight[pl.ds((1 - core) * half, half), origin] = sibling[i]
    far_dk[...] = jnp.zeros_like(far_dk)
    far_dv[...] = jnp.zeros_like(far_dv)
    per_chunk = chunk // (parts * rows)
    total = None
    for c, copy in enumerate(grad_copies):
        copy.wait()
        block = weight[pl.ds(c * per_chunk, per_chunk)].reshape(chunk, width)
        term = dot(grad[c], block, NN)
        total = term if total is None else total + term
    attn_grad[...] = total.astype(BF)

    copies = []
    for g in range(frames // CF):
        mine = pl.ds(g * group_rows, group_rows)
        for h in range(heads):
            cols = pl.ds(h * HD, HD)
            query = queries[pl.ds(g * CF, CF), :, cols].reshape(group_rows, HD)
            prob = probs[g * heads + h]
            out_grad = attn_grad[mine, cols]
            row_dot = jnp.sum(
                out_grad.astype(F32) * attn[mine, cols].astype(F32), axis=1, keepdims=True
            )
            prob_grad = dot(out_grad, value_sets[g, :, cols], NT)
            score_grad = (prob * (prob_grad - row_dot)).astype(BF)
            dq = (dot(score_grad, key_sets[g, :, cols], NN) * (HD**-0.5)).astype(BF)
            query_grad[pl.ds(g * CF, CF), :, cols] = dq.reshape(CF, tokens, HD)
            dk = dot(score_grad, query, TN) * (HD**-0.5)
            dv = dot(prob.astype(BF), out_grad, TN)
            held_dk[mine, cols] = dk[:group_rows]
            held_dv[mine, cols] = dv[:group_rows]
            for e in range(RET):
                owner = lookup[g * RET + e]
                at = slice((CF + e) * tokens, (CF + e + 1) * tokens)
                far_dk[owner, :, cols] += dk[at]
                far_dv[owner, :, cols] += dv[at]
        for which, (held, out) in enumerate(((held_dk, own_dk), (held_dv, own_dv))):
            copy = pltpu.make_async_copy(held.at[mine], out.at[mine], osems.at[g, which])
            copy.start()
            copies.append(copy)
    back[:, 0] = far_dk[...].astype(BF)
    back[:, 1] = far_dv[...].astype(BF)
    for copy in copies:
        copy.wait()


def finish_body(source, came, own_dk, own_dv, key_grad, value_grad, acc_k, acc_v):
    frames, tokens, width = key_grad.shape
    acc_k[...] = own_dk[...].reshape(frames, tokens, width)
    acc_v[...] = own_dv[...].reshape(frames, tokens, width)
    for shard in range(came.shape[0]):
        frame = source[shard]
        acc_k[frame] += came[shard, 0].astype(F32)
        acc_v[frame] += came[shard, 1].astype(F32)
    key_grad[...] = acc_k[...].astype(BF)
    value_grad[...] = acc_v[...].astype(BF)


def per_device(queries, keys, values, out_grad, out_weight, lists):
    frames, tokens, width = queries.shape
    parts, chips = lax.axis_size("dp"), lax.axis_size("y")
    shards, heads = 2 * chips, lax.axis_size("head")
    dp, core = lax.axis_index("dp"), lax.axis_index("core")
    time = ("y", "core")
    myself = lax.axis_index(time)
    rows, entries, groups = frames * tokens, lists.size, frames // CF
    stripe = out_weight.shape[0]
    part_rows, half = stripe // parts, shards // 2
    shape = jax.ShapeDtypeStruct
    dma = pltpu.SemaphoreType.DMA
    other = [(0, 1), (1, 0)]

    grad = lax.all_gather(out_grad.reshape(rows, width), "head", axis=0, tiled=False)

    part = lax.dynamic_slice_in_dim(out_weight, dp * part_rows, part_rows, 0)
    names = jnp.zeros((LIST_ROWS, width), BF).at[0, :entries].set(lists.reshape(entries).astype(BF))
    quarter = lax.all_gather(jnp.concatenate([part, names], axis=0), time, axis=0, tiled=False)
    wanted = quarter[:, part_rows, :entries].astype(jnp.int32)
    source = jnp.max(jnp.where(wanted // frames == myself, wanted % frames, 0), axis=1)
    lookup = lists.reshape(entries) // frames

    packed = pl.pallas_call(
        pack_body,
        out_shape=shape((shards, 2, tokens, width), BF),
        in_specs=[SMEM, VMEM, VMEM],
        out_specs=HBM,
        scratch_shapes=[dma((shards, 2))],
        compiler_params=params(),
        cost_estimate=cost(0, 4 * shards * tokens * width * 2),
        name="pack",
    )(source, keys, values)
    got = lax.all_to_all(packed, time, split_axis=0, concat_axis=0, tiled=True)

    mine = lax.dynamic_slice_in_dim(quarter, core * half, half, 0)[:, :part_rows]
    halves = [
        lax.ppermute(mine, "dp", [(i, (i + s) % parts) for i in range(parts)])
        for s in range(1, parts)
    ]
    got, grad = lax.optimization_barrier((got, grad))
    partial = shape((heads, stripe, width), BF)
    key_rows = (CF + RET) * tokens
    sets = pltpu.VMEM((groups, key_rows, width), BF)
    token_sum = pltpu.VMEM((rows, width), F32)
    far_sum = pltpu.VMEM((shards, tokens, width), F32)
    attn = pl.pallas_call(
        attend_body,
        out_shape=shape((rows, width), BF),
        in_specs=[SMEM] + [VMEM] * 4,
        out_specs=VMEM,
        scratch_shapes=[sets, sets],
        compiler_params=params(),
        cost_estimate=cost(2 * 10**9, 8 * 10**6),
        name="attend",
    )(lookup, queries, keys, values, got)
    attn, *halves = lax.optimization_barrier((attn, *halves))

    def term(side, name):
        return pl.pallas_call(
            term_body,
            out_shape=partial,
            in_specs=[SMEM, VMEM, VMEM],
            out_specs=VMEM,
            compiler_params=params(),
            cost_estimate=cost(3 * 10**9, 3 * 10**6),
            name=name,
        )(side[None], grad, attn)

    send, keep = term(1 - core, "send"), term(core, "keep")
    theirs = lax.ppermute(send, "core", other)
    chip_sum = pl.pallas_call(
        add_body,
        out_shape=partial,
        in_specs=[VMEM, VMEM],
        out_specs=HBM,
        scratch_shapes=[pltpu.VMEM(partial.shape, BF), dma((heads,))],
        compiler_params=params(),
        cost_estimate=cost(10**6, 4 * 10**6),
        name="add",
    )(keep, theirs)
    halves = pl.pallas_call(
        join_body,
        out_shape=shape((parts - 1, half, part_rows, width), BF),
        in_specs=[VMEM] * (parts - 1),
        out_specs=VMEM,
        compiler_params=params(),
        cost_estimate=cost(0, 2 * 10**6),
        name="join",
    )(*halves)
    sibling = lax.ppermute(halves, "core", other)
    weight_grad = lax.psum_scatter(chip_sum, "y", scatter_dimension=0, tiled=False)

    query_grad, back, own_dk, own_dv = pl.pallas_call(
        functools.partial(backward_body, parts),
        out_shape=(
            shape((frames, tokens, width), BF),
            shape((shards, 2, tokens, width), BF),
            shape((rows, width), F32),
            shape((rows, width), F32),
        ),
        in_specs=[SMEM] * 2 + [VMEM] * 5 + [HBM] + [VMEM] * 3,
        out_specs=(VMEM, VMEM, HBM, HBM),
        scratch_shapes=[
            sets,
            sets,
            pltpu.VMEM((groups * width // HD, CF * tokens, key_rows), F32),
            pltpu.VMEM((rows, width), BF),
            pltpu.VMEM((heads, rows, width), BF),
            pltpu.VMEM((shards, parts, part_rows, width), BF),
            far_sum,
            far_sum,
            token_sum,
            token_sum,
            dma((heads,)),
            dma((groups, 2)),
        ],
        compiler_params=params(),
        cost_estimate=cost(6 * 10**9, 9 * 10**6),
        name="backward",
    )(
        lookup, jnp.stack([dp, core]), queries, keys, values, got, attn,
        far(grad), quarter, halves, sibling,
    )
    came = lax.all_to_all(back, time, split_axis=0, concat_axis=0, tiled=True)

    key_grad, value_grad = pl.pallas_call(
        finish_body,
        out_shape=(shape((frames, tokens, width), BF),) * 2,
        in_specs=[SMEM] + [VMEM] * 3,
        out_specs=(VMEM, VMEM),
        scratch_shapes=[pltpu.VMEM((frames, tokens, width), F32)] * 2,
        compiler_params=params(),
        cost_estimate=cost(10**6, 3 * 10**6),
        name="finish",
    )(source, came, own_dk, own_dv)
    return query_grad, key_grad, value_grad, weight_grad.astype(F32)


def solution(mesh):
    dp, time, head = mesh.devices.shape
    fine = jax.sharding.Mesh(
        mesh.devices.reshape(dp, time // 2, 2, head), ("dp", "y", "core", "head")
    )
    tokens = P(("dp", "y", "core"), None, "head")
    return jax.shard_map(
        per_device,
        mesh=fine,
        in_specs=(
            tokens, tokens, tokens, tokens,
            P(("y", "core"), "head"),
            P(("dp", "y", "core"), None),
        ),
        out_specs=(tokens, tokens, tokens, P(("dp", "y", "core"), "head")),
        check_vma=False,
    )
```

```python
import functools

import jax
import jax.numpy as jnp
from jax import lax
from jax.experimental import pallas as pl
from jax.experimental.pallas import tpu as pltpu
from jax.sharding import PartitionSpec as P

HD = 128
CF = 4
RET = 8
LIST_ROWS = 8
BF = jnp.bfloat16
F32 = jnp.float32
HBM = pl.BlockSpec(memory_space=pltpu.HBM)
VMEM = pl.BlockSpec(memory_space=pltpu.VMEM)
SMEM = pl.BlockSpec(memory_space=pltpu.SMEM)
NT = (((1,), (1,)), ((), ()))
NN = (((1,), (0,)), ((), ()))
TN = (((0,), (0,)), ((), ()))


def dot(a, b, dims):
    return lax.dot_general(a, b, dims, preferred_element_type=F32)


def params():
    return pltpu.CompilerParams(vmem_limit_bytes=16 * 1024 * 1024)


def far(array):
    return pltpu.with_memory_space_constraint(array, pltpu.HBM)


def cost(flops, nbytes):
    return pl.CostEstimate(flops=flops, bytes_accessed=nbytes, transcendentals=0)


def pack_body(source, keys, values, out):
    for shard in range(out.shape[0]):
        frame = source[shard]
        out[shard, 0] = keys[frame]
        out[shard, 1] = values[frame]


def fill_sets(lookup, group, keys, values, got, key_set, value_set):
    tokens = keys.shape[1]
    for f in range(CF):
        rows = pl.ds(f * tokens, tokens)
        key_set[rows, :] = keys[group * CF + f]
        value_set[rows, :] = values[group * CF + f]
    for e in range(RET):
        rows = pl.ds((CF + e) * tokens, tokens)
        owner = lookup[group * RET + e]
        key_set[rows, :] = got[owner, 0]
        value_set[rows, :] = got[owner, 1]


def probabilities(query, key_set):
    scores = dot(query, key_set, NT) * (HD**-0.5)
    weighted = jnp.exp(scores - jnp.max(scores, axis=1, keepdims=True))
    return weighted * (1.0 / jnp.sum(weighted, axis=1, keepdims=True))


def attend_body(lookup, queries, keys, values, got, attn, key_sets, value_sets):
    frames, tokens, width = queries.shape
    heads, group_rows = width // HD, CF * tokens
    for g in range(frames // CF):
        fill_sets(lookup, g, keys, values, got, key_sets.at[g], value_sets.at[g])
        for h in range(heads):
            cols = pl.ds(h * HD, HD)
            query = queries[pl.ds(g * CF, CF), :, cols].reshape(group_rows, HD)
            low = probabilities(query, key_sets[g, :, cols]).astype(BF)
            attn[pl.ds(g * group_rows, group_rows), cols] = dot(
                low, value_sets[g, :, cols], NN
            ).astype(BF)


def term_body(side, grad, attn, out):
    stripe = out.shape[1]
    first = side[0] == 0
    for c in range(grad.shape[0]):
        block = jnp.where(first, grad[c, :, :stripe], grad[c, :, stripe:])
        out[c] = dot(block, attn[...], TN).astype(BF)


def add_body(ours, theirs, out, total, sems):
    copies = []
    for c in range(out.shape[0]):
        total[c] = (ours[c].astype(F32) + theirs[c].astype(F32)).astype(BF)
        copy = pltpu.make_async_copy(total.at[c], out.at[c], sems.at[c])
        copy.start()
        copies.append(copy)
    for copy in copies:
        copy.wait()


def join_body(*refs):
    out = refs[-1]
    for i, ref in enumerate(refs[:-1]):
        out[i] = ref[...]


def backward_body(
    parts, lookup, place, queries, keys, values, got, attn, grad_far, quarter, halves, sibling,
    query_grad, back, own_dk, own_dv,
    key_sets, value_sets, probs, attn_grad, grad, weight, far_dk, far_dv, held_dk, held_dv, gsems, osems,
):
    frames, tokens, width = queries.shape
    heads, group_rows = width // HD, CF * tokens
    chunks, _, chunk = grad.shape
    shards, _, rows, _ = weight.shape
    dp, core = place[0], place[1]
    half = shards // 2

    grad_copies = [
        pltpu.make_async_copy(grad_far.at[c], grad.at[c], gsems.at[c]) for c in range(chunks)
    ]
    for copy in grad_copies:
        copy.start()
    for g in range(frames // CF):
        fill_sets(lookup, g, keys, values, got, key_sets.at[g], value_sets.at[g])
        for h in range(heads):
            cols = pl.ds(h * HD, HD)
            query = queries[pl.ds(g * CF, CF), :, cols].reshape(group_rows, HD)
            probs[g * heads + h] = probabilities(query, key_sets[g, :, cols])
    weight[:, dp] = quarter[:, :rows]
    for i in range(parts - 1):
        origin = lax.rem(dp + parts - (1 + i), parts)
        weight[pl.ds(core * half, half), origin] = halves[i]
        weight[pl.ds((1 - core) * half, half), origin] = sibling[i]
    far_dk[...] = jnp.zeros_like(far_dk)
    far_dv[...] = jnp.zeros_like(far_dv)
    per_chunk = chunk // (parts * rows)
    total = None
    for c, copy in enumerate(grad_copies):
        copy.wait()
        block = weight[pl.ds(c * per_chunk, per_chunk)].reshape(chunk, width)
        term = dot(grad[c], block, NN)
        total = term if total is None else total + term
    attn_grad[...] = total.astype(BF)

    copies = []
    for g in range(frames // CF):
        mine = pl.ds(g * group_rows, group_rows)
        for h in range(heads):
            cols = pl.ds(h * HD, HD)
            query = queries[pl.ds(g * CF, CF), :, cols].reshape(group_rows, HD)
            prob = probs[g * heads + h]
            out_grad = attn_grad[mine, cols]
            row_dot = jnp.sum(
                out_grad.astype(F32) * attn[mine, cols].astype(F32), axis=1, keepdims=True
            )
            prob_grad = dot(out_grad, value_sets[g, :, cols], NT)
            score_grad = (prob * (prob_grad - row_dot)).astype(BF)
            dq = (dot(score_grad, key_sets[g, :, cols], NN) * (HD**-0.5)).astype(BF)
            query_grad[pl.ds(g * CF, CF), :, cols] = dq.reshape(CF, tokens, HD)
            dk = dot(score_grad, query, TN) * (HD**-0.5)
            dv = dot(prob.astype(BF), out_grad, TN)
            held_dk[mine, cols] = dk[:group_rows]
            held_dv[mine, cols] = dv[:group_rows]
            for e in range(RET):
                owner = lookup[g * RET + e]
                at = slice((CF + e) * tokens, (CF + e + 1) * tokens)
                far_dk[owner, :, cols] += dk[at]
                far_dv[owner, :, cols] += dv[at]
        for which, (held, out) in enumerate(((held_dk, own_dk), (held_dv, own_dv))):
            copy = pltpu.make_async_copy(held.at[mine], out.at[mine], osems.at[g, which])
            copy.start()
            copies.append(copy)
    back[:, 0] = far_dk[...].astype(BF)
    back[:, 1] = far_dv[...].astype(BF)
    for copy in copies:
        copy.wait()


def finish_body(source, came, own_dk, own_dv, key_grad, value_grad, acc_k, acc_v):
    frames, tokens, width = key_grad.shape
    acc_k[...] = own_dk[...].reshape(frames, tokens, width)
    acc_v[...] = own_dv[...].reshape(frames, tokens, width)
    for shard in range(came.shape[0]):
        frame = source[shard]
        acc_k[frame] += came[shard, 0].astype(F32)
        acc_v[frame] += came[shard, 1].astype(F32)
    key_grad[...] = acc_k[...].astype(BF)
    value_grad[...] = acc_v[...].astype(BF)


def per_device(queries, keys, values, out_grad, out_weight, lists):
    frames, tokens, width = queries.shape
    parts, chips = lax.axis_size("dp"), lax.axis_size("y")
    shards, heads = 2 * chips, lax.axis_size("head")
    dp, core = lax.axis_index("dp"), lax.axis_index("core")
    time = ("y", "core")
    myself = lax.axis_index(time)
    rows, entries, groups = frames * tokens, lists.size, frames // CF
    stripe = out_weight.shape[0]
    part_rows, half = stripe // parts, shards // 2
    shape = jax.ShapeDtypeStruct
    dma = pltpu.SemaphoreType.DMA
    other = [(0, 1), (1, 0)]

    grad = lax.all_gather(out_grad.reshape(rows, width), "head", axis=0, tiled=False)

    part = lax.dynamic_slice_in_dim(out_weight, dp * part_rows, part_rows, 0)
    names = jnp.zeros((LIST_ROWS, width), BF).at[0, :entries].set(lists.reshape(entries).astype(BF))
    quarter = lax.all_gather(jnp.concatenate([part, names], axis=0), time, axis=0, tiled=False)
    wanted = quarter[:, part_rows, :entries].astype(jnp.int32)
    source = jnp.max(jnp.where(wanted // frames == myself, wanted % frames, 0), axis=1)
    lookup = lists.reshape(entries) // frames

    packed = pl.pallas_call(
        pack_body,
        out_shape=shape((shards, 2, tokens, width), BF),
        in_specs=[SMEM, VMEM, VMEM],
        out_specs=VMEM,
        compiler_params=params(),
        cost_estimate=cost(0, 4 * shards * tokens * width * 2),
        name="pack",
    )(source, keys, values)
    got = lax.all_to_all(packed, time, split_axis=0, concat_axis=0, tiled=True)

    mine = lax.dynamic_slice_in_dim(quarter, core * half, half, 0)[:, :part_rows]
    halves = [
        lax.ppermute(mine, "dp", [(i, (i + s) % parts) for i in range(parts)])
        for s in range(1, parts)
    ]
    got, grad = lax.optimization_barrier((got, grad))
    partial = shape((heads, stripe, width), BF)
    key_rows = (CF + RET) * tokens
    sets = pltpu.VMEM((groups, key_rows, width), BF)
    token_sum = pltpu.VMEM((rows, width), F32)
    far_sum = pltpu.VMEM((shards, tokens, width), F32)
    attn = pl.pallas_call(
        attend_body,
        out_shape=shape((rows, width), BF),
        in_specs=[SMEM] + [VMEM] * 4,
        out_specs=VMEM,
        scratch_shapes=[sets, sets],
        compiler_params=params(),
        cost_estimate=cost(2 * 10**9, 8 * 10**6),
        name="attend",
    )(lookup, queries, keys, values, got)
    attn, *halves = lax.optimization_barrier((attn, *halves))

    def term(side, name):
        return pl.pallas_call(
            term_body,
            out_shape=partial,
            in_specs=[SMEM, VMEM, VMEM],
            out_specs=VMEM,
            compiler_params=params(),
            cost_estimate=cost(3 * 10**9, 3 * 10**6),
            name=name,
        )(side[None], grad, attn)

    send, keep = term(1 - core, "send"), term(core, "keep")
    theirs = lax.ppermute(send, "core", other)
    chip_sum = pl.pallas_call(
        add_body,
        out_shape=partial,
        in_specs=[VMEM, VMEM],
        out_specs=HBM,
        scratch_shapes=[pltpu.VMEM(partial.shape, BF), dma((heads,))],
        compiler_params=params(),
        cost_estimate=cost(10**6, 4 * 10**6),
        name="add",
    )(keep, theirs)
    halves = pl.pallas_call(
        join_body,
        out_shape=shape((parts - 1, half, part_rows, width), BF),
        in_specs=[VMEM] * (parts - 1),
        out_specs=VMEM,
        compiler_params=params(),
        cost_estimate=cost(0, 2 * 10**6),
        name="join",
    )(*halves)
    sibling = lax.ppermute(halves, "core", other)
    weight_grad = lax.psum_scatter(chip_sum, "y", scatter_dimension=0, tiled=False)

    query_grad, back, own_dk, own_dv = pl.pallas_call(
        functools.partial(backward_body, parts),
        out_shape=(
            shape((frames, tokens, width), BF),
            shape((shards, 2, tokens, width), BF),
            shape((rows, width), F32),
            shape((rows, width), F32),
        ),
        in_specs=[SMEM] * 2 + [VMEM] * 5 + [HBM] + [VMEM] * 3,
        out_specs=(VMEM, VMEM, HBM, HBM),
        scratch_shapes=[
            sets,
            sets,
            pltpu.VMEM((groups * width // HD, CF * tokens, key_rows), F32),
            pltpu.VMEM((rows, width), BF),
            pltpu.VMEM((heads, rows, width), BF),
            pltpu.VMEM((shards, parts, part_rows, width), BF),
            far_sum,
            far_sum,
            token_sum,
            token_sum,
            dma((heads,)),
            dma((groups, 2)),
        ],
        compiler_params=params(),
        cost_estimate=cost(6 * 10**9, 9 * 10**6),
        name="backward",
    )(
        lookup, jnp.stack([dp, core]), queries, keys, values, got, attn,
        far(grad), quarter, halves, sibling,
    )
    came = lax.all_to_all(back, time, split_axis=0, concat_axis=0, tiled=True)

    key_grad, value_grad = pl.pallas_call(
        finish_body,
        out_shape=(shape((frames, tokens, width), BF),) * 2,
        in_specs=[SMEM] + [VMEM] * 3,
        out_specs=(VMEM, VMEM),
        scratch_shapes=[pltpu.VMEM((frames, tokens, width), F32)] * 2,
        compiler_params=params(),
        cost_estimate=cost(10**6, 3 * 10**6),
        name="finish",
    )(source, came, own_dk, own_dv)
    return query_grad, key_grad, value_grad, weight_grad.astype(F32)


def solution(mesh):
    dp, time, head = mesh.devices.shape
    fine = jax.sharding.Mesh(
        mesh.devices.reshape(dp, time // 2, 2, head), ("dp", "y", "core", "head")
    )
    tokens = P(("dp", "y", "core"), None, "head")
    return jax.shard_map(
        per_device,
        mesh=fine,
        in_specs=(
            tokens, tokens, tokens, tokens,
            P(("y", "core"), "head"),
            P(("dp", "y", "core"), None),
        ),
        out_specs=(tokens, tokens, tokens, P(("dp", "y", "core"), "head")),
        check_vma=False,
    )
```

```python
import functools

import jax
import jax.numpy as jnp
from jax import lax
from jax.experimental import pallas as pl
from jax.experimental.pallas import tpu as pltpu
from jax.sharding import PartitionSpec as P

HD = 128
CF = 4
RET = 8
LIST_ROWS = 8
BF = jnp.bfloat16
F32 = jnp.float32
HBM = pl.BlockSpec(memory_space=pltpu.HBM)
VMEM = pl.BlockSpec(memory_space=pltpu.VMEM)
SMEM = pl.BlockSpec(memory_space=pltpu.SMEM)
NT = (((1,), (1,)), ((), ()))
NN = (((1,), (0,)), ((), ()))
TN = (((0,), (0,)), ((), ()))


def dot(a, b, dims):
    return lax.dot_general(a, b, dims, preferred_element_type=F32)


def params():
    return pltpu.CompilerParams(vmem_limit_bytes=16 * 1024 * 1024)


def far(array):
    return pltpu.with_memory_space_constraint(array, pltpu.HBM)


def cost(flops, nbytes):
    return pl.CostEstimate(flops=flops, bytes_accessed=nbytes, transcendentals=0)


def pack_body(source, keys, values, out, own_keys, own_values):
    for shard in range(out.shape[0]):
        frame = source[shard]
        out[shard, 0] = keys[frame]
        out[shard, 1] = values[frame]
    own_keys[...] = keys[...]
    own_values[...] = values[...]


def fill_sets(lookup, group, keys, values, got, key_set, value_set):
    tokens = keys.shape[1]
    for f in range(CF):
        rows = pl.ds(f * tokens, tokens)
        key_set[rows, :] = keys[group * CF + f]
        value_set[rows, :] = values[group * CF + f]
    for e in range(RET):
        rows = pl.ds((CF + e) * tokens, tokens)
        owner = lookup[group * RET + e]
        key_set[rows, :] = got[owner, 0]
        value_set[rows, :] = got[owner, 1]


def probabilities(query, key_set):
    scores = dot(query, key_set, NT) * (HD**-0.5)
    weighted = jnp.exp(scores - jnp.max(scores, axis=1, keepdims=True))
    return weighted * (1.0 / jnp.sum(weighted, axis=1, keepdims=True))


def attend_body(lookup, queries, keys, values, got, attn, key_sets, value_sets):
    frames, tokens, width = queries.shape
    heads, group_rows = width // HD, CF * tokens
    for g in range(frames // CF):
        fill_sets(lookup, g, keys, values, got, key_sets.at[g], value_sets.at[g])
        for h in range(heads):
            cols = pl.ds(h * HD, HD)
            query = queries[pl.ds(g * CF, CF), :, cols].reshape(group_rows, HD)
            low = probabilities(query, key_sets[g, :, cols]).astype(BF)
            attn[pl.ds(g * group_rows, group_rows), cols] = dot(
                low, value_sets[g, :, cols], NN
            ).astype(BF)


def term_body(side, grad, attn, out):
    stripe = out.shape[1]
    first = side[0] == 0
    for c in range(grad.shape[0]):
        block = jnp.where(first, grad[c, :, :stripe], grad[c, :, stripe:])
        out[c] = dot(block, attn[...], TN).astype(BF)


def add_body(ours, theirs, out, total, sems):
    copies = []
    for c in range(out.shape[0]):
        total[c] = (ours[c].astype(F32) + theirs[c].astype(F32)).astype(BF)
        copy = pltpu.make_async_copy(total.at[c], out.at[c], sems.at[c])
        copy.start()
        copies.append(copy)
    for copy in copies:
        copy.wait()


def join_body(*refs):
    out = refs[-1]
    for i, ref in enumerate(refs[:-1]):
        out[i] = ref[...]


def backward_body(
    parts, lookup, place, queries, keys, values, got, attn, grad_far, quarter, halves, sibling,
    query_grad, back, own_dk, own_dv,
    key_sets, value_sets, probs, attn_grad, grad, weight, far_dk, far_dv, held_dk, held_dv, gsems, osems,
):
    frames, tokens, width = queries.shape
    heads, group_rows = width // HD, CF * tokens
    chunks, _, chunk = grad.shape
    shards, _, rows, _ = weight.shape
    dp, core = place[0], place[1]
    half = shards // 2

    grad_copies = [
        pltpu.make_async_copy(grad_far.at[c], grad.at[c], gsems.at[c]) for c in range(chunks)
    ]
    for copy in grad_copies:
        copy.start()
    for g in range(frames // CF):
        fill_sets(lookup, g, keys, values, got, key_sets.at[g], value_sets.at[g])
        for h in range(heads):
            cols = pl.ds(h * HD, HD)
            query = queries[pl.ds(g * CF, CF), :, cols].reshape(group_rows, HD)
            probs[g * heads + h] = probabilities(query, key_sets[g, :, cols])
    weight[:, dp] = quarter[:, :rows]
    for i in range(parts - 1):
        origin = lax.rem(dp + parts - (1 + i), parts)
        weight[pl.ds(core * half, half), origin] = halves[i]
        weight[pl.ds((1 - core) * half, half), origin] = sibling[i]
    far_dk[...] = jnp.zeros_like(far_dk)
    far_dv[...] = jnp.zeros_like(far_dv)
    per_chunk = chunk // (parts * rows)
    total = None
    for c, copy in enumerate(grad_copies):
        copy.wait()
        block = weight[pl.ds(c * per_chunk, per_chunk)].reshape(chunk, width)
        term = dot(grad[c], block, NN)
        total = term if total is None else total + term
    attn_grad[...] = total.astype(BF)

    copies = []
    for g in range(frames // CF):
        mine = pl.ds(g * group_rows, group_rows)
        for h in range(heads):
            cols = pl.ds(h * HD, HD)
            query = queries[pl.ds(g * CF, CF), :, cols].reshape(group_rows, HD)
            prob = probs[g * heads + h]
            out_grad = attn_grad[mine, cols]
            row_dot = jnp.sum(
                out_grad.astype(F32) * attn[mine, cols].astype(F32), axis=1, keepdims=True
            )
            prob_grad = dot(out_grad, value_sets[g, :, cols], NT)
            score_grad = (prob * (prob_grad - row_dot)).astype(BF)
            dq = (dot(score_grad, key_sets[g, :, cols], NN) * (HD**-0.5)).astype(BF)
            query_grad[pl.ds(g * CF, CF), :, cols] = dq.reshape(CF, tokens, HD)
            dk = dot(score_grad, query, TN) * (HD**-0.5)
            dv = dot(prob.astype(BF), out_grad, TN)
            held_dk[mine, cols] = dk[:group_rows]
            held_dv[mine, cols] = dv[:group_rows]
            for e in range(RET):
                owner = lookup[g * RET + e]
                at = slice((CF + e) * tokens, (CF + e + 1) * tokens)
                far_dk[owner, :, cols] += dk[at]
                far_dv[owner, :, cols] += dv[at]
        for which, (held, out) in enumerate(((held_dk, own_dk), (held_dv, own_dv))):
            copy = pltpu.make_async_copy(held.at[mine], out.at[mine], osems.at[g, which])
            copy.start()
            copies.append(copy)
    back[:, 0] = far_dk[...].astype(BF)
    back[:, 1] = far_dv[...].astype(BF)
    for copy in copies:
        copy.wait()


def finish_body(source, came, own_dk, own_dv, key_grad, value_grad, acc_k, acc_v):
    frames, tokens, width = key_grad.shape
    acc_k[...] = own_dk[...].reshape(frames, tokens, width)
    acc_v[...] = own_dv[...].reshape(frames, tokens, width)
    for shard in range(came.shape[0]):
        frame = source[shard]
        acc_k[frame] += came[shard, 0].astype(F32)
        acc_v[frame] += came[shard, 1].astype(F32)
    key_grad[...] = acc_k[...].astype(BF)
    value_grad[...] = acc_v[...].astype(BF)


def per_device(queries, keys, values, out_grad, out_weight, lists):
    frames, tokens, width = queries.shape
    parts, chips = lax.axis_size("dp"), lax.axis_size("y")
    shards, heads = 2 * chips, lax.axis_size("head")
    dp, core = lax.axis_index("dp"), lax.axis_index("core")
    time = ("y", "core")
    myself = lax.axis_index(time)
    rows, entries, groups = frames * tokens, lists.size, frames // CF
    stripe = out_weight.shape[0]
    part_rows, half = stripe // parts, shards // 2
    shape = jax.ShapeDtypeStruct
    dma = pltpu.SemaphoreType.DMA
    other = [(0, 1), (1, 0)]

    grad = lax.all_gather(out_grad.reshape(rows, width), "head", axis=0, tiled=False)

    part = lax.dynamic_slice_in_dim(out_weight, dp * part_rows, part_rows, 0)
    names = jnp.zeros((LIST_ROWS, width), BF).at[0, :entries].set(lists.reshape(entries).astype(BF))
    quarter = lax.all_gather(jnp.concatenate([part, names], axis=0), time, axis=0, tiled=False)
    wanted = quarter[:, part_rows, :entries].astype(jnp.int32)
    source = jnp.max(jnp.where(wanted // frames == myself, wanted % frames, 0), axis=1)
    lookup = lists.reshape(entries) // frames

    packed, keys, values = pl.pallas_call(
        pack_body,
        out_shape=(shape((shards, 2, tokens, width), BF),)
        + (shape((frames, tokens, width), BF),) * 2,
        in_specs=[SMEM, VMEM, VMEM],
        out_specs=(VMEM,) * 3,
        compiler_params=params(),
        cost_estimate=cost(0, 4 * shards * tokens * width * 2),
        name="pack",
    )(source, keys, values)
    got = lax.all_to_all(packed, time, split_axis=0, concat_axis=0, tiled=True)

    mine = lax.dynamic_slice_in_dim(quarter, core * half, half, 0)[:, :part_rows]
    halves = [
        lax.ppermute(mine, "dp", [(i, (i + s) % parts) for i in range(parts)])
        for s in range(1, parts)
    ]
    got, grad = lax.optimization_barrier((got, grad))
    partial = shape((heads, stripe, width), BF)
    key_rows = (CF + RET) * tokens
    sets = pltpu.VMEM((groups, key_rows, width), BF)
    token_sum = pltpu.VMEM((rows, width), F32)
    far_sum = pltpu.VMEM((shards, tokens, width), F32)
    attn = pl.pallas_call(
        attend_body,
        out_shape=shape((rows, width), BF),
        in_specs=[SMEM] + [VMEM] * 4,
        out_specs=VMEM,
        scratch_shapes=[sets, sets],
        compiler_params=params(),
        cost_estimate=cost(2 * 10**9, 8 * 10**6),
        name="attend",
    )(lookup, queries, keys, values, got)
    attn, *halves = lax.optimization_barrier((attn, *halves))

    def term(side, name):
        return pl.pallas_call(
            term_body,
            out_shape=partial,
            in_specs=[SMEM, VMEM, VMEM],
            out_specs=VMEM,
            compiler_params=params(),
            cost_estimate=cost(3 * 10**9, 3 * 10**6),
            name=name,
        )(side[None], grad, attn)

    send, keep = term(1 - core, "send"), term(core, "keep")
    theirs = lax.ppermute(send, "core", other)
    chip_sum = pl.pallas_call(
        add_body,
        out_shape=partial,
        in_specs=[VMEM, VMEM],
        out_specs=HBM,
        scratch_shapes=[pltpu.VMEM(partial.shape, BF), dma((heads,))],
        compiler_params=params(),
        cost_estimate=cost(10**6, 4 * 10**6),
        name="add",
    )(keep, theirs)
    halves = pl.pallas_call(
        join_body,
        out_shape=shape((parts - 1, half, part_rows, width), BF),
        in_specs=[VMEM] * (parts - 1),
        out_specs=VMEM,
        compiler_params=params(),
        cost_estimate=cost(0, 2 * 10**6),
        name="join",
    )(*halves)
    sibling = lax.ppermute(halves, "core", other)
    weight_grad = lax.psum_scatter(chip_sum, "y", scatter_dimension=0, tiled=False)

    query_grad, back, own_dk, own_dv = pl.pallas_call(
        functools.partial(backward_body, parts),
        out_shape=(
            shape((frames, tokens, width), BF),
            shape((shards, 2, tokens, width), BF),
            shape((rows, width), F32),
            shape((rows, width), F32),
        ),
        in_specs=[SMEM] * 2 + [VMEM] * 5 + [HBM] + [VMEM] * 3,
        out_specs=(VMEM, VMEM, HBM, HBM),
        scratch_shapes=[
            sets,
            sets,
            pltpu.VMEM((groups * width // HD, CF * tokens, key_rows), F32),
            pltpu.VMEM((rows, width), BF),
            pltpu.VMEM((heads, rows, width), BF),
            pltpu.VMEM((shards, parts, part_rows, width), BF),
            far_sum,
            far_sum,
            token_sum,
            token_sum,
            dma((heads,)),
            dma((groups, 2)),
        ],
        compiler_params=params(),
        cost_estimate=cost(6 * 10**9, 9 * 10**6),
        name="backward",
    )(
        lookup, jnp.stack([dp, core]), queries, keys, values, got, attn,
        far(grad), quarter, halves, sibling,
    )
    came = lax.all_to_all(back, time, split_axis=0, concat_axis=0, tiled=True)

    key_grad, value_grad = pl.pallas_call(
        finish_body,
        out_shape=(shape((frames, tokens, width), BF),) * 2,
        in_specs=[SMEM] + [VMEM] * 3,
        out_specs=(VMEM, VMEM),
        scratch_shapes=[pltpu.VMEM((frames, tokens, width), F32)] * 2,
        compiler_params=params(),
        cost_estimate=cost(10**6, 3 * 10**6),
        name="finish",
    )(source, came, own_dk, own_dv)
    return query_grad, key_grad, value_grad, weight_grad.astype(F32)


def solution(mesh):
    dp, time, head = mesh.devices.shape
    fine = jax.sharding.Mesh(
        mesh.devices.reshape(dp, time // 2, 2, head), ("dp", "y", "core", "head")
    )
    tokens = P(("dp", "y", "core"), None, "head")
    return jax.shard_map(
        per_device,
        mesh=fine,
        in_specs=(
            tokens, tokens, tokens, tokens,
            P(("y", "core"), "head"),
            P(("dp", "y", "core"), None),
        ),
        out_specs=(tokens, tokens, tokens, P(("dp", "y", "core"), "head")),
        check_vma=False,
    )
```
